256 devices in a mesh: dp: 16 (over x_lo, z), seq: 16 (over y, x_hi, core).
Axes of the slice: x: 4 (x_hi: 2, x_lo: 2; x = x_hi * 2 + x_lo), y: 4, z: 8, core: 2. Of those that a mesh axis runs over, the one named last changes fastest.
Arguments:
- queries: bfloat16 [32, 1024, 2048], P('dp', 'seq'), may hold values from -200 to 200
- keys: bfloat16 [32, 1024, 2048], P('dp', 'seq'), may hold values from -8 to 8, as said below
- values: bfloat16 [32, 1024, 2048], P('dp', 'seq'), may hold values from -100 to 100, as said below
- out_grad: bfloat16 [32, 1024, 2048], P('dp', 'seq'), may hold values from -6 to 6
- conv_weight: float32 [7, 2048], replicated, may hold values from -3 to 3
- conv_bias: float32 [2048], replicated, may hold values from -3 to 3
- gain: float32 [2048], replicated, may hold values from 0.1 to 1.9
Outputs:
- query_grad: bfloat16 [32, 1024, 2048], P('dp', 'seq')
- key_grad: bfloat16 [32, 1024, 2048], P('dp', 'seq')
- value_grad: bfloat16 [32, 1024, 2048], P('dp', 'seq')
- weight_grad: float32 [7, 2048], P(None, 'seq')
- bias_grad: float32 [2048], P('seq')
- gain_grad: float32 [2048], P('seq')
The draws below stay inside these ranges and needn't reach their ends.
Inputs may be any that keep to these rules, and one draw needn't show every extreme that they name: keys of order one. values scaled by a factor for each frame and one for each channel.
All inputs are finite; a program needn't handle non-finite values.
Results may differ from the reference program's by a relative error of at most 0.024.
Values may be sent and summed in bfloat16 or wider, within the bound.
No kernel may reach another device: no remote copies, remote signals or barrier semaphores. Data moves between devices by JAX's collectives and lax.ppermute only.
A program may use at most 64 MiB of HBM per device.

```python
import math
import jax
import jax.numpy as jnp
from jax import lax

HDIM = 128
KERNEL = 7
LEN = 1024
C = 2048
BATCH = 32
HALF = 3


def key_field(key, twin_weight):
    raw = jnp.clip(jax.random.normal(jax.random.fold_in(key, 11), (BATCH, LEN, C), jnp.float32), -6.0, 6.0)
    noise = jnp.clip(jax.random.normal(jax.random.fold_in(key, 12), (BATCH, LEN, C), jnp.float32), -3.0, 3.0)
    frame = lax.broadcasted_iota(jnp.int32, (BATCH, LEN, C), 1)
    paired = jnp.where(frame % 97 == 5, twin_weight, 0.0)
    earlier = jnp.roll(raw, 1, axis=1)
    return raw + paired * (earlier + 0.1 * noise - raw)


def draw_keys(key, part):
    field = key_field(key, 0.0)
    return field.astype(jnp.bfloat16)


def draw_queries(key, part):
    key = jax.random.fold_in(key, 3)
    result = 0.9 * jnp.clip(jax.random.normal(key, (BATCH, LEN, C), jnp.float32), -6.0, 6.0)
    return result.astype(jnp.bfloat16)


def draw_values(key, part):
    key = jax.random.fold_in(key, 5)
    rows = jnp.exp(jax.random.uniform(jax.random.fold_in(key, 6), (BATCH, LEN, 1), jnp.float32, jnp.log(0.5), jnp.log(5.0)))
    columns = jnp.exp(jax.random.uniform(jax.random.fold_in(key, 7), (1, 1, C), jnp.float32, jnp.log(0.3), jnp.log(3.0)))
    noise = jnp.clip(jax.random.normal(key, (BATCH, LEN, C), jnp.float32), -6.0, 6.0)
    return (noise * rows * columns).astype(jnp.bfloat16)


def strengthened(drawn, stream_key, source, target, blocks, factor):
    def block_of(position):
        return (jnp.arange(drawn.shape[position]) // (drawn.shape[position] // blocks)).reshape((-1,) + (1,) * (drawn.ndim - 1 - position))

    near = jax.random.permutation(stream_key, blocks)[block_of(target)]
    second = (block_of(target) + blocks // 2) % blocks
    return jnp.where((block_of(source) == near) | (block_of(source) == second), factor * drawn, drawn)


def block_levels(rng, extent, pieces, least, high):
    level, own = 1.0, jax.random.fold_in(rng, 6)
    for dim, shards_of in pieces:
        steps = jnp.exp(jax.random.uniform(jax.random.fold_in(own, dim), (shards_of,), jnp.float32, least / len(pieces), high / len(pieces)))
        level = level * jnp.repeat(steps, extent[dim] // shards_of).reshape([-1 if axis == dim else 1 for axis in range(len(extent))])
    return level


def gaussian(stream_key, shape, deviation, limit, cuts=(), kind=jnp.bfloat16):
    loudness = block_levels(stream_key, shape, cuts, -0.22, 0.18) if cuts else 1.0
    values = jax.random.normal(stream_key, shape, jnp.float32) * deviation * loudness
    return jnp.minimum(jnp.maximum(values, -limit), limit).astype(kind)


def heavy_noise(own_key, shape, width, limit, pieces, heavy, kind=jnp.bfloat16):
    values = width * jax.random.normal(own_key, shape, jnp.float32)
    if pieces:
        values = values * block_levels(own_key, shape, pieces, -0.22, 0.18)
    return jnp.clip(strengthened(values, jax.random.fold_in(own_key, 3), *heavy), -limit, limit).astype(kind)


def setup_inputs(seed: int = 0) -> dict:
    key_list = jax.random.split(jax.random.key(seed), 8)
    queries = draw_queries(jax.random.fold_in(key_list[7], 71), 0)
    keys = draw_keys(jax.random.fold_in(key_list[7], 71), 0)
    values = draw_values(jax.random.fold_in(key_list[7], 71), 0)
    out_grad = heavy_noise(key_list[3], (BATCH, LEN, C), 1.0, 6.0, ((0, 16), (1, 16)), (0, 2, 16, 2.0))
    conv_weight = gaussian(key_list[4], (KERNEL, C), 0.5, 3.0, (), jnp.float32)
    conv_bias = gaussian(key_list[5], (C,), 0.5, 3.0, (), jnp.float32)
    gain = jnp.clip(1.0 + 0.18 * jax.random.normal(key_list[6], (C,), jnp.float32), 0.1, 1.9)
    return dict(queries=queries, keys=keys, values=values, out_grad=out_grad, conv_weight=conv_weight, conv_bias=conv_bias, gain=gain)


def split_heads(x):
    return x.astype(jnp.float32).reshape(x.shape[0], -1, HDIM)

def attend_forward(items):
    query, key, value = items
    scale = 1.0 / math.sqrt(HDIM)
    scores = jnp.einsum('qhd,khd->hqk', split_heads(query), split_heads(key)) * scale
    top = lax.optimization_barrier(jnp.max(scores, axis=-1, keepdims=True))
    lse = top + jnp.log(lax.optimization_barrier(jnp.sum(jnp.exp(scores - top), axis=-1, keepdims=True)))
    weights = jnp.exp(scores - lse).astype(jnp.bfloat16)
    out = jnp.einsum('hqk,khd->qhd', weights.astype(jnp.float32), split_heads(value))
    return out.reshape(query.shape[0], -1).astype(jnp.bfloat16)

def attend_backward(items):
    query, key, value, grad = items
    scale = 1.0 / math.sqrt(HDIM)
    qf, kf, vf, gf = (split_heads(query), split_heads(key), split_heads(value), split_heads(grad))
    scores = jnp.einsum('qhd,khd->hqk', qf, kf) * scale
    top = lax.optimization_barrier(jnp.max(scores, axis=-1, keepdims=True))
    lse = top + jnp.log(lax.optimization_barrier(jnp.sum(jnp.exp(scores - top), axis=-1, keepdims=True)))
    probs = jnp.exp(scores - lse)
    weights = probs.astype(jnp.bfloat16).astype(jnp.float32)
    value_grad = jnp.einsum('hqk,qhd->khd', weights, gf)
    prob_grad = jnp.einsum('qhd,khd->hqk', gf, vf)
    delta = lax.optimization_barrier(jnp.sum(probs * prob_grad, axis=-1, keepdims=True))
    score_grad = (probs * (prob_grad - delta)).astype(jnp.bfloat16).astype(jnp.float32)
    query_grad = jnp.einsum('hqk,khd->qhd', score_grad, kf) * scale
    key_grad = jnp.einsum('hqk,qhd->khd', score_grad, qf) * scale
    rows = query.shape[0]
    return (query_grad.reshape(rows, -1).astype(jnp.bfloat16), key_grad.reshape(rows, -1).astype(jnp.bfloat16), value_grad.reshape(rows, -1).astype(jnp.bfloat16))

def reference(queries, keys, values, out_grad, conv_weight, conv_bias, gain):
    attended = lax.map(attend_forward, (queries, keys, values))

    def branch(items):
        frames, upstream = items
        padded = jnp.pad(frames.astype(jnp.float32), ((HALF, HALF), (0, 0)))
        conv = conv_bias[None, :] + sum((conv_weight[t][None, :] * padded[t:t + LEN] for t in range(KERNEL)))
        ratio = lax.rsqrt(lax.optimization_barrier(jnp.mean(conv * conv, axis=-1, keepdims=True)) + 1e-06)
        upper = upstream.astype(jnp.float32)
        gain_term = lax.optimization_barrier(jnp.sum(upper * conv * ratio, axis=0))
        dot = lax.optimization_barrier(jnp.mean(conv * gain[None, :] * upper, axis=-1, keepdims=True))
        conv_grad = ratio * gain[None, :] * upper - conv * ratio ** 3 * dot
        bias_term = lax.optimization_barrier(jnp.sum(conv_grad, axis=0))
        weight_term = jnp.stack([lax.optimization_barrier(jnp.sum(conv_grad * padded[t:t + LEN], axis=0)) for t in range(KERNEL)])
        grad_pad = jnp.pad(conv_grad, ((HALF, HALF), (0, 0)))
        back = sum((conv_weight[t][None, :] * grad_pad[2 * HALF - t:2 * HALF - t + LEN] for t in range(KERNEL)))
        return ((upper + back).astype(jnp.bfloat16), weight_term, bias_term, gain_term)
    attended_grad, weight_terms, bias_terms, gain_terms = lax.map(branch, (attended, out_grad))
    query_grad, key_grad, value_grad = lax.map(attend_backward, (queries, keys, values, attended_grad))
    return (query_grad, key_grad, value_grad, lax.optimization_barrier(jnp.sum(weight_terms, axis=0)), lax.optimization_barrier(jnp.sum(bias_terms, axis=0)), lax.optimization_barrier(jnp.sum(gain_terms, axis=0)))
```

```python
import functools
import math

import jax
import jax.numpy as jnp
from jax import lax
from jax.experimental import pallas as pl
from jax.experimental.pallas import tpu as pltpu
from jax.sharding import PartitionSpec as P

HDIM = 128
SUB = 8
HEADS = 2
TAPS = 7
HALF = TAPS // 2
ROWS = 16
BLOCK = 256
LIMIT = 56 * 1024 * 1024
EPS = 1e-06

NT = (((1,), (1,)), ((), ()))
TN = (((0,), (0,)), ((), ()))


def dot(a, b, dims=(((1,), (0,)), ((), ()))):
    return lax.dot_general(a, b, dims, preferred_element_type=jnp.float32)


def pack_kernel(*refs):
    *sources, packed = refs
    for a, ref in enumerate(sources):
        for x in range(2):
            for core in range(2):
                for hh in range(HEADS):
                    lane = (hh * 2 + core) * HDIM
                    packed[x * 2 + core, a, hh] = ref[x, :, lane : lane + HDIM]


def unpack_kernel(packed, *results):
    for a, ref in enumerate(results):
        for x in range(2):
            for core in range(2):
                for hh in range(HEADS):
                    lane = (hh * 2 + core) * HDIM
                    ref[x, :, lane : lane + HDIM] = packed[x * 2 + core, a, hh]


def pack(arrays, seq):
    count = len(arrays)
    _, frames, width = arrays[0].shape
    steps = seq // 4
    return pl.pallas_call(
        pack_kernel,
        grid=(steps,),
        in_specs=[pl.BlockSpec((2, frames, width // steps), lambda i: (0, 0, i))] * count,
        out_specs=pl.BlockSpec((4, count, HEADS, frames, HDIM), lambda i: (i, 0, 0, 0, 0)),
        out_shape=jax.ShapeDtypeStruct((seq, count, HEADS, frames, HDIM), arrays[0].dtype),
        compiler_params=pltpu.CompilerParams(vmem_limit_bytes=LIMIT),
        name="pack",
    )(*arrays)


def unpack(packed, width):
    seq, count, _, frames, _ = packed.shape
    steps = seq // 4
    return pl.pallas_call(
        unpack_kernel,
        grid=(steps,),
        in_specs=[pl.BlockSpec((4, count, HEADS, frames, HDIM), lambda i: (i, 0, 0, 0, 0))],
        out_specs=[pl.BlockSpec((2, frames, width // steps), lambda i: (0, 0, i))] * count,
        out_shape=[jax.ShapeDtypeStruct((2, frames, width), packed.dtype)] * count,
        compiler_params=pltpu.CompilerParams(vmem_limit_bytes=LIMIT),
        name="unpack",
    )(packed)


def shifted_ends(padded, h, groups):
    sublane = lax.broadcasted_iota(jnp.int32, (SUB, HDIM), 0)
    for j in range(HALF):
        last = padded[h, (groups + j) * SUB : (groups + j + 1) * SUB, :]
        padded[h, j * SUB : (j + 1) * SUB, :] = jnp.where(
            sublane == 0, 0.0, pltpu.roll(last, 1, axis=0)
        )
    for j in range(HALF):
        first = padded[h, (HALF + j) * SUB : (HALF + j + 1) * SUB, :]
        padded[h, (HALF + groups + j) * SUB : (HALF + groups + j + 1) * SUB, :] = jnp.where(
            sublane == SUB - 1, 0.0, pltpu.roll(first, SUB - 1, axis=0)
        )


def forward_kernel(peers, recv, params, exps, outs, invs, att, conv, upper, stats):
    seq, _, _, frames, _ = recv.shape
    length = seq * frames
    groups = length // SUB
    scale = math.log2(math.e) / math.sqrt(HDIM)
    per_block = BLOCK // frames
    for h in range(HEADS):
        key = recv[:, 1, h].reshape(length, HDIM)
        value = recv[:, 2, h].reshape(length, HDIM)
        wide = jnp.concatenate([value, jnp.ones_like(value)], axis=1)
        for b in range(length // BLOCK):
            rows = slice(b * BLOCK, (b + 1) * BLOCK)
            query = recv[b * per_block : (b + 1) * per_block, 0, h].reshape(BLOCK, HDIM)
            scores = dot(query, key, NT)
            top = jnp.max(scores, axis=-1, keepdims=True)
            weights = jnp.exp2((scores - top) * scale).astype(jnp.bfloat16)
            exps[h, rows, :] = weights
            sums = dot(weights, wide)
            inv = 1.0 / sums[:, HDIM:]
            out = sums[:, :HDIM] * inv
            outs[h, rows, :] = out
            invs[h, rows, :] = inv
            rounded = out.astype(jnp.bfloat16).astype(jnp.float32)
            for j in range(BLOCK // groups):
                s = b * (BLOCK // groups) + j
                att[h, pl.ds(HALF * SUB + s, groups, stride=SUB), :] = rounded[
                    j * groups : (j + 1) * groups
                ]
        grad = recv[:, 3, h].reshape(length, HDIM).astype(jnp.float32)
        for s in range(SUB):
            upper[h, pl.ds(s, groups, stride=SUB), :] = grad[s * groups : (s + 1) * groups]
        shifted_ends(att, h, groups)

    lane = lax.broadcasted_iota(jnp.int32, (SUB, HDIM), 1)
    step = 16

    def some(i, carry):
        sumsq, dots = carry
        base = pl.multiple_of(i * step * SUB, step * SUB)
        total_sq = jnp.zeros((step * SUB, HDIM), jnp.float32)
        total_dot = jnp.zeros((step * SUB, HDIM), jnp.float32)
        for h in range(HEADS):
            par = params[h]
            value = par[TAPS][None, :]
            for t in range(TAPS):
                value = value + par[t][None, :] * att[h, pl.ds(base + t * SUB, step * SUB), :]
            conv[h, pl.ds(base, step * SUB), :] = value
            total_sq = total_sq + value * value
            total_dot = total_dot + value * (
                par[TAPS + 1][None, :] * upper[h, pl.ds(base, step * SUB), :]
            )
        sq = jnp.sum(total_sq, axis=-1, keepdims=True)
        dt = jnp.sum(total_dot, axis=-1, keepdims=True)
        for j in range(step):
            here = lane == i * step + j
            sumsq = jnp.where(here, sq[j * SUB : (j + 1) * SUB], sumsq)
            dots = jnp.where(here, dt[j * SUB : (j + 1) * SUB], dots)
        return sumsq, dots

    zero = jnp.zeros((SUB, HDIM), jnp.float32)
    sumsq, dots = lax.fori_loop(0, groups // step, some, (zero, zero))
    for p in range(peers):
        stats[p, :SUB, :] = sumsq
        stats[p, SUB:, :] = dots


def backward_kernel(
    width, stats, recv, params, exps, outs, invs, att, conv, upper, packed, part, cgrad, agrad, nat, sgrad
):
    seq, _, _, frames, _ = recv.shape
    length = seq * frames
    groups = length // SUB
    scale = 1.0 / math.sqrt(HDIM)
    total = jnp.sum(stats[...], axis=0)
    ratio = lax.rsqrt(total[:SUB] / width + EPS)
    beta = ratio * ratio * ratio * (total[SUB:] / width)
    zero = jnp.zeros((SUB, HDIM), jnp.float32)
    bias_sum, gain_sum = [zero] * HEADS, [zero] * HEADS
    gains = [jnp.broadcast_to(params[h, TAPS + 1][None, :], (SUB, HDIM)) for h in range(HEADS)]
    for r in range(groups):
        own = slice(r * SUB, (r + 1) * SUB)
        ratio_r = jnp.broadcast_to(ratio[:, r : r + 1], (SUB, HDIM))
        beta_r = jnp.broadcast_to(beta[:, r : r + 1], (SUB, HDIM))
        for h in range(HEADS):
            value, up = conv[h, own, :], upper[h, own, :]
            scaled = ratio_r * up
            grad = gains[h] * scaled - value * beta_r
            gain_sum[h] = gain_sum[h] + scaled * value
            bias_sum[h] = bias_sum[h] + grad
            cgrad[h, (HALF + r) * SUB : (HALF + r + 1) * SUB, :] = grad
    step = 8
    for h in range(HEADS):
        shifted_ends(cgrad, h, groups)
        par = params[h]

        def some(i, carry):
            base = pl.multiple_of(i * step * SUB, step * SUB)
            back = upper[h, pl.ds(base, step * SUB), :]
            own = cgrad[h, pl.ds(base + HALF * SUB, step * SUB), :]
            sums = []
            for t in range(TAPS):
                back = back + par[t][None, :] * cgrad[
                    h, pl.ds(base + (2 * HALF - t) * SUB, step * SUB), :
                ]
                term = own * att[h, pl.ds(base + t * SUB, step * SUB), :]
                sums.append(carry[t] + jnp.sum(term.reshape(step, SUB, HDIM), axis=0))
            agrad[pl.ds(base, step * SUB), :] = back
            return tuple(sums)

        taps = lax.fori_loop(0, groups // step, some, (zero,) * TAPS)
        for t in range(TAPS):
            part[h, t : t + 1, :] = jnp.sum(taps[t], axis=0, keepdims=True)
        part[h, TAPS : TAPS + 1, :] = jnp.sum(bias_sum[h], axis=0, keepdims=True)
        part[h, TAPS + 1 : TAPS + 2, :] = jnp.sum(gain_sum[h], axis=0, keepdims=True)
        part[h, TAPS + 2 :, :] = jnp.zeros((ROWS - TAPS - 2, HDIM), jnp.float32)
        for s in range(SUB):
            nat[s * groups : (s + 1) * groups, :] = agrad[pl.ds(s, groups, stride=SUB), :].astype(
                jnp.bfloat16
            )

        query = recv[:, 0, h].reshape(length, HDIM)
        key = recv[:, 1, h].reshape(length, HDIM)
        value = recv[:, 2, h].reshape(length, HDIM)
        inv = invs[h]
        per_block = BLOCK // frames
        for b in range(length // BLOCK):
            rows = slice(b * BLOCK, (b + 1) * BLOCK)
            grad = nat[rows, :]
            prob_grad = dot(grad, value, NT)
            delta = jnp.sum(grad.astype(jnp.float32) * outs[h, rows, :], axis=-1, keepdims=True)
            score_grad = (exps[h, rows, :].astype(jnp.float32) * (prob_grad - delta)).astype(
                jnp.bfloat16
            )
            sgrad[rows, :] = score_grad
            result = dot(score_grad, key) * (inv[rows] * scale)
            packed[b * per_block : (b + 1) * per_block, 0, h] = result.astype(jnp.bfloat16).reshape(
                per_block, frames, HDIM
            )
        scaled_query = (query.astype(jnp.float32) * inv).astype(jnp.bfloat16)
        key_grad = dot(sgrad[...], scaled_query, TN) * scale
        packed[:, 1, h] = key_grad.astype(jnp.bfloat16).reshape(seq, frames, HDIM)
        scaled_grad = (nat[...].astype(jnp.float32) * inv).astype(jnp.bfloat16)
        value_grad = dot(exps[h], scaled_grad, TN)
        packed[:, 2, h] = value_grad.astype(jnp.bfloat16).reshape(seq, frames, HDIM)


def in_vmem(shape, dtype):
    return pltpu.VMEM(shape, dtype)


def held(count):
    return [pl.BlockSpec(memory_space=pltpu.VMEM)] * count


def forward(recv, params, peers):
    seq, _, _, frames, _ = recv.shape
    length = seq * frames
    shapes = [
        ((HEADS, length, length), jnp.bfloat16),
        ((HEADS, length, HDIM), jnp.float32),
        ((HEADS, length, HDIM), jnp.float32),
        ((HEADS, length + 2 * HALF * SUB, HDIM), jnp.float32),
        ((HEADS, length, HDIM), jnp.float32),
        ((HEADS, length, HDIM), jnp.float32),
        ((peers, 2 * SUB, HDIM), jnp.float32),
    ]
    return pl.pallas_call(
        functools.partial(forward_kernel, peers),
        in_specs=held(2),
        out_specs=held(len(shapes)),
        out_shape=[jax.ShapeDtypeStruct(*s) for s in shapes],
        compiler_params=pltpu.CompilerParams(vmem_limit_bytes=LIMIT),
        name="forward",
    )(recv, params)


def backward(width, stats, recv, params, saved):
    seq, _, _, frames, _ = recv.shape
    length = seq * frames
    return pl.pallas_call(
        functools.partial(backward_kernel, width),
        in_specs=held(3 + len(saved)),
        out_specs=held(2),
        out_shape=[
            jax.ShapeDtypeStruct((seq, 3, HEADS, frames, HDIM), jnp.bfloat16),
            jax.ShapeDtypeStruct((HEADS, ROWS, HDIM), jnp.float32),
        ],
        scratch_shapes=[
            pltpu.VMEM((HEADS, length + 2 * HALF * SUB, HDIM), jnp.float32),
            pltpu.VMEM((length, HDIM), jnp.float32),
            pltpu.VMEM((length, HDIM), jnp.bfloat16),
            pltpu.VMEM((length, length), jnp.bfloat16),
        ],
        compiler_params=pltpu.CompilerParams(vmem_limit_bytes=LIMIT),
        name="backward",
    )(stats, recv, params, *saved)


def exchange(x, groups=None):
    return lax.all_to_all(
        x, "seq", split_axis=0, concat_axis=0, tiled=True, axis_index_groups=groups
    )


def own_params(conv_weight, conv_bias, gain, y, core):
    rows = jnp.concatenate([conv_weight, conv_bias[None], gain[None]], axis=0)
    rows = jnp.pad(rows, ((0, ROWS - rows.shape[0]), (0, 0)))
    rows = rows.reshape(ROWS, -1, HEADS, 2, HDIM)
    rows = lax.dynamic_index_in_dim(rows, y, axis=1, keepdims=False)
    rows = lax.dynamic_index_in_dim(rows, core, axis=2, keepdims=False)
    return rows.transpose(1, 0, 2)


def sum_params(part, x, seq, dp):
    own = lax.dynamic_index_in_dim(part, x, axis=0, keepdims=False)
    other = lax.dynamic_index_in_dim(part, 1 - x, axis=0, keepdims=False)
    total = own + lax.ppermute(other, "seq", [(i, i ^ 2) for i in range(seq)])
    shift = dp // 2
    shifts = [shift] + [1 << i for i in range(shift.bit_length() - 1)]
    for shift in shifts:
        total = total + lax.ppermute(total, "dp", [(i, i ^ shift) for i in range(dp)])
    return total


def per_device(queries, keys, values, out_grad, conv_weight, conv_bias, gain):
    width = queries.shape[2]
    seq, dp = lax.axis_size("seq"), lax.axis_size("dp")
    index = lax.axis_index("seq")
    y, x, core = index // 4, (index // 2) % 2, index % 2
    same_x = [[b * 4 + a * 2 + c for b in range(seq // 4) for c in range(2)] for a in range(2)]
    params = own_params(conv_weight, conv_bias, gain, y, core)
    recv = exchange(pack((queries, keys, values, out_grad), seq))
    *saved, stats = forward(recv, params, len(same_x[0]))
    stats = exchange(stats, same_x)
    packed, part = backward(width, stats, recv, params, saved)
    total = sum_params(part, x, seq, dp)
    query_grad, key_grad, value_grad = unpack(exchange(packed), width)
    return (query_grad, key_grad, value_grad, total[:TAPS], total[TAPS], total[TAPS + 1])


def solution(mesh):
    frames = P("dp", "seq", None)
    return jax.shard_map(
        per_device,
        mesh=mesh,
        in_specs=(frames, frames, frames, frames, P(), P(), P()),
        out_specs=(frames, frames, frames, P(None, "seq"), P("seq"), P("seq")),
        check_vma=False,
    )
```

```python
import functools
import math

import jax
import jax.numpy as jnp
from jax import lax
from jax.experimental import pallas as pl
from jax.experimental.pallas import tpu as pltpu
from jax.sharding import PartitionSpec as P

HDIM = 128
SUB = 8
HEADS = 2
TAPS = 7
HALF = TAPS // 2
ROWS = 16
BLOCK = 256
LIMIT = 24 * 1024 * 1024
EPS = 1e-06

NT = (((1,), (1,)), ((), ()))
TN = (((0,), (0,)), ((), ()))


def dot(a, b, dims=(((1,), (0,)), ((), ()))):
    return lax.dot_general(a, b, dims, preferred_element_type=jnp.float32)


def pack_kernel(*refs):
    *sources, result, packed, sems, done = refs
    for y in range(packed.shape[0]):
        for a, ref in enumerate(sources):
            for core in range(2):
                for hh in range(HEADS):
                    lane = ((y * HEADS + hh) * 2 + core) * HDIM
                    pltpu.make_async_copy(
                        ref.at[:, :, lane : lane + HDIM], packed.at[y, :, core, a, hh], sems.at[y]
                    ).start()
    for y in range(packed.shape[0]):
        pltpu.make_async_copy(packed.at[y], packed.at[y], sems.at[y]).wait()
        pltpu.make_async_copy(packed.at[y], result.at[y], done).start()
    pltpu.make_async_copy(packed, result, done).wait()


def unpack_kernel(*refs):
    packed, *results, sem = refs
    for a, ref in enumerate(results):
        for y in range(packed.shape[0]):
            for core in range(2):
                for hh in range(HEADS):
                    lane = ((y * HEADS + hh) * 2 + core) * HDIM
                    pltpu.make_async_copy(
                        packed.at[y, :, core, a, hh], ref.at[:, :, lane : lane + HDIM], sem
                    ).start()
    pltpu.make_async_copy(packed, packed, sem).wait()


def pack(arrays, seq):
    count = len(arrays)
    _, frames, _ = arrays[0].shape
    packed = pl.pallas_call(
        pack_kernel,
        in_specs=[pl.BlockSpec(memory_space=pltpu.HBM)] * count,
        out_specs=pl.BlockSpec(memory_space=pltpu.HBM),
        out_shape=pltpu.HBM((seq // 4, 2, 2, count, HEADS, frames, HDIM), arrays[0].dtype),
        scratch_shapes=[
            pltpu.VMEM((seq // 4, 2, 2, count, HEADS, frames, HDIM), arrays[0].dtype),
            pltpu.SemaphoreType.DMA((seq // 4,)),
            pltpu.SemaphoreType.DMA,
        ],
        compiler_params=pltpu.CompilerParams(vmem_limit_bytes=LIMIT),
        name="pack",
    )(*[pltpu.with_memory_space_constraint(a, pltpu.HBM) for a in arrays])
    return packed.reshape(seq, count, HEADS, frames, HDIM)


def unpack(packed, width):
    seq, count, _, frames, _ = packed.shape
    return pl.pallas_call(
        unpack_kernel,
        in_specs=[pl.BlockSpec(memory_space=pltpu.VMEM)],
        out_specs=[pl.BlockSpec(memory_space=pltpu.HBM)] * count,
        out_shape=[pltpu.HBM((2, frames, width), packed.dtype)] * count,
        scratch_shapes=[pltpu.SemaphoreType.DMA],
        compiler_params=pltpu.CompilerParams(vmem_limit_bytes=LIMIT),
        name="unpack",
    )(*resident(packed.reshape(seq // 4, 2, 2, count, HEADS, frames, HDIM)))


def shifted_ends(padded, h, groups):
    sublane = lax.broadcasted_iota(jnp.int32, (SUB, HDIM), 0)
    for j in range(HALF):
        last = padded[h, (groups + j) * SUB : (groups + j + 1) * SUB, :]
        padded[h, j * SUB : (j + 1) * SUB, :] = jnp.where(
            sublane == 0, 0.0, pltpu.roll(last, 1, axis=0)
        )
    for j in range(HALF):
        first = padded[h, (HALF + j) * SUB : (HALF + j + 1) * SUB, :]
        padded[h, (HALF + groups + j) * SUB : (HALF + groups + j + 1) * SUB, :] = jnp.where(
            sublane == SUB - 1, 0.0, pltpu.roll(first, SUB - 1, axis=0)
        )


def turn(target, offset, natural):
    groups = natural.shape[0] // SUB
    for s in range(SUB):
        target[pl.ds(offset + s, groups, stride=SUB), :] = natural[s * groups : (s + 1) * groups]


def convolve(att, h, par, base, count):
    value = par[TAPS][None, :]
    for t in range(TAPS):
        value = value + par[t][None, :] * att[h, pl.ds(base + t * SUB, count), :]
    return value


def forward_kernel(
    peers, recv, params, exps_out, invs_out, outs, stats, exps, invs, upper, att, sems
):
    seq, _, _, frames, _ = recv.shape
    length = seq * frames
    groups = length // SUB
    scale = math.log2(math.e) / math.sqrt(HDIM)
    per_block = BLOCK // frames
    for h in range(HEADS):
        key = recv[:, 1, h].reshape(length, HDIM)
        value = recv[:, 2, h].reshape(length, HDIM)
        wide = jnp.concatenate([value, jnp.ones_like(value)], axis=1)
        for b in range(length // BLOCK):
            rows = slice(b * BLOCK, (b + 1) * BLOCK)
            query = recv[b * per_block : (b + 1) * per_block, 0, h].reshape(BLOCK, HDIM)
            scores = dot(query, key, NT)
            top = jnp.max(scores, axis=-1, keepdims=True)
            weights = jnp.exp2((scores - top) * scale).astype(jnp.bfloat16)
            exps[h, rows, :] = weights
            pltpu.make_async_copy(exps.at[h, rows], exps_out.at[h, rows], sems.at[0]).start()
            sums = dot(weights, wide)
            inv = 1.0 / sums[:, HDIM:]
            out = sums[:, :HDIM] * inv
            outs[h, rows, :] = out
            invs[h, rows, :] = inv
            rounded = out.astype(jnp.bfloat16).astype(jnp.float32)
            for j in range(BLOCK // groups):
                s = b * (BLOCK // groups) + j
                att[h, pl.ds(HALF * SUB + s, groups, stride=SUB), :] = rounded[
                    j * groups : (j + 1) * groups
                ]
        pltpu.make_async_copy(invs.at[h], invs_out.at[h], sems.at[1]).start()
        turn(upper.at[h], 0, recv[:, 3, h].reshape(length, HDIM).astype(jnp.float32))
        shifted_ends(att, h, groups)

    lane = lax.broadcasted_iota(jnp.int32, (SUB, HDIM), 1)
    step = 16

    def some(i, carry):
        sumsq, dots = carry
        base = pl.multiple_of(i * step * SUB, step * SUB)
        total_sq = jnp.zeros((step * SUB, HDIM), jnp.float32)
        total_dot = jnp.zeros((step * SUB, HDIM), jnp.float32)
        for h in range(HEADS):
            par = params[h]
            value = convolve(att, h, par, base, step * SUB)
            total_sq = total_sq + value * value
            total_dot = total_dot + value * (
                par[TAPS + 1][None, :] * upper[h, pl.ds(base, step * SUB), :]
            )
        sq = jnp.sum(total_sq, axis=-1, keepdims=True)
        dt = jnp.sum(total_dot, axis=-1, keepdims=True)
        for j in range(step):
            here = lane == i * step + j
            sumsq = jnp.where(here, sq[j * SUB : (j + 1) * SUB], sumsq)
            dots = jnp.where(here, dt[j * SUB : (j + 1) * SUB], dots)
        return sumsq, dots

    zero = jnp.zeros((SUB, HDIM), jnp.float32)
    sumsq, dots = lax.fori_loop(0, groups // step, some, (zero, zero))
    for p in range(peers):
        stats[p, :SUB, :] = sumsq
        stats[p, SUB:, :] = dots
    for i, (src, dst) in enumerate(((exps, exps_out), (invs, invs_out))):
        pltpu.make_async_copy(src, dst, sems.at[i]).wait()


def norm_kernel(
    width, stats, recv, params, outs, exps_in, invs_in, grads, part, exps, invs, cgrad, agrad, upper, att, sems
):
    seq, _, _, frames, _ = recv.shape
    length = seq * frames
    groups = length // SUB
    fetches = [
        pltpu.make_async_copy(invs_in, invs, sems.at[0]),
        pltpu.make_async_copy(exps_in.at[0], exps.at[0], sems.at[1]),
        pltpu.make_async_copy(exps_in.at[1], exps.at[1], sems.at[2]),
    ]
    for fetch in fetches:
        fetch.start()
    total = jnp.sum(stats[...], axis=0)
    ratio = lax.rsqrt(total[:SUB] / width + EPS)
    beta = ratio * ratio * ratio * (total[SUB:] / width)
    zero = jnp.zeros((SUB, HDIM), jnp.float32)
    bias_sum, gain_sum = [zero] * HEADS, [zero] * HEADS
    gains = [jnp.broadcast_to(params[h, TAPS + 1][None, :], (SUB, HDIM)) for h in range(HEADS)]
    for h in range(HEADS):
        turn(upper.at[h], 0, recv[:, 3, h].reshape(length, HDIM).astype(jnp.float32))
        turn(att.at[h], HALF * SUB, outs[h].astype(jnp.bfloat16).astype(jnp.float32))
        shifted_ends(att, h, groups)
    for r in range(groups):
        own = slice(r * SUB, (r + 1) * SUB)
        ratio_r = jnp.broadcast_to(ratio[:, r : r + 1], (SUB, HDIM))
        beta_r = jnp.broadcast_to(beta[:, r : r + 1], (SUB, HDIM))
        for h in range(HEADS):
            value, up = convolve(att, h, params[h], r * SUB, SUB), upper[h, own, :]
            scaled = ratio_r * up
            grad = gains[h] * scaled - value * beta_r
            gain_sum[h] = gain_sum[h] + scaled * value
            bias_sum[h] = bias_sum[h] + grad
            cgrad[h, (HALF + r) * SUB : (HALF + r + 1) * SUB, :] = grad
    step = 8
    for h in range(HEADS):
        shifted_ends(cgrad, h, groups)
        par = params[h]

        def some(i, carry):
            base = pl.multiple_of(i * step * SUB, step * SUB)
            back = upper[h, pl.ds(base, step * SUB), :]
            own = cgrad[h, pl.ds(base + HALF * SUB, step * SUB), :]
            sums = []
            for t in range(TAPS):
                back = back + par[t][None, :] * cgrad[
                    h, pl.ds(base + (2 * HALF - t) * SUB, step * SUB), :
                ]
                term = own * att[h, pl.ds(base + t * SUB, step * SUB), :]
                sums.append(carry[t] + jnp.sum(term.reshape(step, SUB, HDIM), axis=0))
            agrad[pl.ds(base, step * SUB), :] = back
            return tuple(sums)

        taps = lax.fori_loop(0, groups // step, some, (zero,) * TAPS)
        for t in range(TAPS):
            part[h, t : t + 1, :] = jnp.sum(taps[t], axis=0, keepdims=True)
        part[h, TAPS : TAPS + 1, :] = jnp.sum(bias_sum[h], axis=0, keepdims=True)
        part[h, TAPS + 1 : TAPS + 2, :] = jnp.sum(gain_sum[h], axis=0, keepdims=True)
        part[h, TAPS + 2 :, :] = jnp.zeros((ROWS - TAPS - 2, HDIM), jnp.float32)
        if h == 0:
            fetches[0].wait()
        for s in range(SUB):
            rows = slice(s * groups, (s + 1) * groups)
            grads[h, rows, :] = (agrad[pl.ds(s, groups, stride=SUB), :] * invs[h, rows, :]).astype(
                jnp.bfloat16
            )
    for fetch in fetches[1:]:
        fetch.wait()


def backward_kernel(recv, grads, exps, outs, packed_out, sgrad, packed, sent):
    seq, _, _, frames, _ = recv.shape
    length = seq * frames
    scale = 1.0 / math.sqrt(HDIM)
    per_block = BLOCK // frames
    for h in range(HEADS):
        query = recv[:, 0, h].reshape(length, HDIM)
        key = recv[:, 1, h].reshape(length, HDIM)
        value = recv[:, 2, h].reshape(length, HDIM)
        for b in range(length // BLOCK):
            rows = slice(b * BLOCK, (b + 1) * BLOCK)
            grad = grads[h, rows, :]
            prob_grad = dot(grad, value, NT)
            delta = jnp.sum(grad.astype(jnp.float32) * outs[h, rows, :], axis=-1, keepdims=True)
            score_grad = (exps[h, rows, :].astype(jnp.float32) * (prob_grad - delta)).astype(
                jnp.bfloat16
            )
            sgrad[rows, :] = score_grad
            result = dot(score_grad, key) * scale
            packed[0, h, b * per_block : (b + 1) * per_block] = result.astype(jnp.bfloat16).reshape(
                per_block, frames, HDIM
            )
        pltpu.make_async_copy(packed.at[0, h], packed_out.at[:, 0, h], sent).start()
        key_grad = dot(sgrad[...], query, TN) * scale
        packed[1, h] = key_grad.astype(jnp.bfloat16).reshape(seq, frames, HDIM)
        pltpu.make_async_copy(packed.at[1, h], packed_out.at[:, 1, h], sent).start()
        value_grad = dot(exps[h], grads[h], TN)
        packed[2, h] = value_grad.astype(jnp.bfloat16).reshape(seq, frames, HDIM)
        pltpu.make_async_copy(packed.at[2, h], packed_out.at[:, 2, h], sent).start()
    pltpu.make_async_copy(packed, packed, sent).wait()


def resident(*arrays):
    return [pltpu.with_memory_space_constraint(a, pltpu.VMEM) for a in arrays]


def held(count, space=pltpu.VMEM):
    return [pl.BlockSpec(memory_space=space)] * count


def forward(recv, params, peers):
    seq, _, _, frames, _ = recv.shape
    length = seq * frames
    exps = (HEADS, length, length), jnp.bfloat16
    rows = (HEADS, length, HDIM), jnp.float32
    return pl.pallas_call(
        functools.partial(forward_kernel, peers),
        in_specs=held(2),
        out_specs=held(2, pltpu.HBM) + held(2),
        out_shape=[
            pltpu.HBM(*exps),
            pltpu.HBM(*rows),
            pltpu.VMEM(*rows),
            pltpu.VMEM((peers, 2 * SUB, HDIM), jnp.float32),
        ],
        scratch_shapes=[
            pltpu.VMEM(*exps),
            pltpu.VMEM(*rows),
            pltpu.VMEM(*rows),
            pltpu.VMEM((HEADS, length + 2 * HALF * SUB, HDIM), jnp.float32),
            pltpu.SemaphoreType.DMA((2,)),
        ],
        compiler_params=pltpu.CompilerParams(vmem_limit_bytes=LIMIT),
        name="forward",
    )(*resident(recv, params))


def norm(width, stats, recv, params, outs, exps, invs):
    seq, _, _, frames, _ = recv.shape
    length = seq * frames
    padded = pltpu.VMEM((HEADS, length + 2 * HALF * SUB, HDIM), jnp.float32)
    return pl.pallas_call(
        functools.partial(norm_kernel, width),
        in_specs=held(4) + held(2, pltpu.HBM),
        out_specs=held(3),
        out_shape=[
            pltpu.VMEM((HEADS, length, HDIM), jnp.bfloat16),
            pltpu.VMEM((HEADS, ROWS, HDIM), jnp.float32),
            pltpu.VMEM(exps.shape, exps.dtype),
        ],
        scratch_shapes=[
            pltpu.VMEM(invs.shape, invs.dtype),
            padded,
            pltpu.VMEM((length, HDIM), jnp.float32),
            pltpu.VMEM((HEADS, length, HDIM), jnp.float32),
            padded,
            pltpu.SemaphoreType.DMA((3,)),
        ],
        compiler_params=pltpu.CompilerParams(vmem_limit_bytes=LIMIT),
        name="norm",
    )(
        *resident(stats, recv, params, outs),
        *[pltpu.with_memory_space_constraint(a, pltpu.HBM) for a in (exps, invs)],
    )


def backward(recv, grads, exps, outs):
    seq, _, _, frames, _ = recv.shape
    length = seq * frames
    return pl.pallas_call(
        backward_kernel,
        in_specs=held(4),
        out_specs=pl.BlockSpec(memory_space=pltpu.HBM),
        out_shape=pltpu.HBM((seq, 3, HEADS, frames, HDIM), jnp.bfloat16),
        scratch_shapes=[
            pltpu.VMEM((length, length), jnp.bfloat16),
            pltpu.VMEM((3, HEADS, seq, frames, HDIM), jnp.bfloat16),
            pltpu.SemaphoreType.DMA,
        ],
        compiler_params=pltpu.CompilerParams(vmem_limit_bytes=LIMIT),
        cost_estimate=pl.CostEstimate(
            flops=16 * HEADS * length * length * HDIM, bytes_accessed=1 << 24, transcendentals=0
        ),
        name="backward",
    )(*resident(recv, grads, exps, outs))


def exchange(x, groups=None):
    return lax.all_to_all(
        x, "seq", split_axis=0, concat_axis=0, tiled=True, axis_index_groups=groups
    )


def own_params(conv_weight, conv_bias, gain, y, core):
    rows = jnp.concatenate([conv_weight, conv_bias[None], gain[None]], axis=0)
    rows = jnp.pad(rows, ((0, ROWS - rows.shape[0]), (0, 0)))
    rows = rows.reshape(ROWS, -1, HEADS, 2, HDIM)
    rows = lax.dynamic_index_in_dim(rows, y, axis=1, keepdims=False)
    rows = lax.dynamic_index_in_dim(rows, core, axis=2, keepdims=False)
    return rows.transpose(1, 0, 2)


def sum_pair(part, x, seq):
    own = lax.dynamic_index_in_dim(part, x, axis=0, keepdims=False)
    other = lax.dynamic_index_in_dim(part, 1 - x, axis=0, keepdims=False)
    return own + lax.ppermute(other, "seq", [(i, i ^ 2) for i in range(seq)])


def sum_dp(total, dp):
    for bit in range(dp.bit_length() - 1):
        total = total + lax.ppermute(total, "dp", [(i, i ^ (1 << bit)) for i in range(dp)])
    return total


def per_device(queries, keys, values, out_grad, conv_weight, conv_bias, gain):
    width = queries.shape[2]
    seq, dp = lax.axis_size("seq"), lax.axis_size("dp")
    index = lax.axis_index("seq")
    y, x, core = index // 4, (index // 2) % 2, index % 2
    same_x = [[b * 4 + a * 2 + c for b in range(seq // 4) for c in range(2)] for a in range(2)]
    params = own_params(conv_weight, conv_bias, gain, y, core)
    recv = exchange(pack((queries, keys, values, out_grad), seq))
    exps, invs, outs, stats = forward(recv, params, len(same_x[0]))
    stats = exchange(stats, same_x)
    grads, part, exps = norm(width, stats, recv, params, outs, exps, invs)
    total = sum_pair(part, x, seq)
    packed = backward(recv, grads, exps, outs)
    packed, total = lax.optimization_barrier((packed, total))
    total = sum_dp(total, dp)
    query_grad, key_grad, value_grad = unpack(exchange(packed), width)
    return (query_grad, key_grad, value_grad, total[:TAPS], total[TAPS], total[TAPS + 1])


def solution(mesh):
    frames = P("dp", "seq", None)
    return jax.shard_map(
        per_device,
        mesh=mesh,
        in_specs=(frames, frames, frames, frames, P(), P(), P()),
        out_specs=(frames, frames, frames, P(None, "seq"), P("seq"), P("seq")),
        check_vma=False,
    )
```
